32 devices in a mesh: grp: 4 (over z), dir: 8 (over y, x, core).
Axes of the slice: x: 2, y: 2, z: 4, core: 2. Of those that a mesh axis runs over, the one named last changes fastest.
Arguments:
- incident: float32 [4, 256, 256, 128], P(None, ('grp', 'dir')), may hold values from -6 to 6
- currents_past: bfloat16 [2, 256, 256, 128], P(None, ('grp', 'dir')), may hold values from -6 to 6
- spectra_past: bfloat16 [2, 32, 1152, 128], P(None, ('grp', 'dir')), may hold values from -9 to 9
- self_inverse: bfloat16 [256, 256, 256], P(('grp', 'dir')), may hold values from -0.25 to 0.25
- near_blocks: bfloat16 [256, 6, 2, 256, 256], P(('grp', 'dir')), may hold values from -0.078125 to 0.078125
- neighbours: int32 [256, 6], P(('grp', 'dir')), may hold values from 0 to 255, as said below
- near_mask: int32 [256, 6], P(('grp', 'dir')), may hold values 0 or 1
- ray_out: bfloat16 [256, 1152], replicated, may hold values from -0.375 to 0.375
- ray_in: bfloat16 [1152, 256], replicated, may hold values from -0.1875 to 0.1875
- child_shift: float32 [8, 1152], replicated, may hold values from -1 to 1
- far_sources: int32 [32, 16], replicated, may hold values from 0 to 31
- far_delays: int32 [32, 16], replicated, may hold values from 1 to 2
- translation: float32 [32, 16, 1152], P(None, None, ('grp', 'dir')), may hold values from -0.75 to 0.75
Outputs:
- currents: bfloat16 [4, 256, 256, 128], P(None, ('grp', 'dir'))
The draws below stay inside these ranges and needn't reach their ends.
Inputs may be any that keep to these rules, and one draw needn't show every extreme that they name: `neighbours`: the entry of group g names a group held by the same device as g, by the device just before it or by the one just after it, devices counted in the order grp then dir, each holding 8 consecutive groups.
All inputs are finite; a program needn't handle non-finite values. No bound on the sum of `near_mask` on one device may be relied on, other than what follows from the above.
Results may differ from the reference program's by a relative error of at most 0.0095.
Values may be sent and summed in bfloat16 or wider, within the bound.
A program may use at most 128 MiB of HBM per device.

```python
import jax
import jax.numpy as jnp
from jax import lax

E = 256
K = 1152
R = 128
CH = 8
NEAR = 6
LAGS = 2
F = 16
STEPS = 4
G_DEV = 8
GROUPS = 256
PARENTS = 32


def draw_neighbours(key, part):
    key_device, key_slot = jax.random.split(key)
    owner = jnp.arange(GROUPS, dtype=jnp.int32)[:, None] // G_DEV
    offset = jax.random.randint(key_device, (GROUPS, NEAR), -1, 2)
    device = jnp.clip(owner + offset, 0, GROUPS // G_DEV - 1)
    member = jax.random.randint(key_slot, (GROUPS, NEAR), 0, G_DEV)
    chosen = (device * G_DEV + member).astype(jnp.int32)
    chosen = chosen.at[0, 0].set(0)
    chosen = chosen.at[GROUPS - 1, 0].set(GROUPS - 1)
    return chosen.astype(jnp.int32)


def set_ends(array, rng, least, largest):
    longest = array.shape.index(max(array.shape))
    spots = []
    for shift in (0, 1):
        where = [jax.random.randint(jax.random.fold_in(rng, axis), (), 0, length) for axis, length in enumerate(array.shape)]
        where[longest] = (where[longest] + shift) % array.shape[longest]
        spots.append(tuple(where))
    return array.at[spots[0]].set(least).at[spots[1]].set(largest)


def block_scale(stream_key, dims, cuts, low, top_value):
    level, own = 1.0, jax.random.fold_in(stream_key, 6)
    for dim, blocks in cuts:
        heights = jnp.exp(jax.random.uniform(jax.random.fold_in(own, dim), (blocks,), jnp.float32, low / len(cuts), top_value / len(cuts)))
        level = level * jnp.repeat(heights, dims[dim] // blocks).reshape([-1 if axis == dim else 1 for axis in range(len(dims))])
    return level


def noise(own_key, extent, scale, bound, cuts=(), kind=jnp.bfloat16):
    drawn = jax.random.normal(own_key, extent, jnp.float32) * scale
    if len(cuts) > 0:
        drawn = block_scale(own_key, extent, cuts, -0.22, 0.18) * drawn
    return jnp.clip(drawn, min=-bound, max=bound).astype(kind)


def setup_inputs(seed: int = 0) -> dict:
    keys = jax.random.split(jax.random.key(seed), 14)
    return {
        "incident": noise(keys[0], (STEPS, GROUPS, E, R), 1.0, 6.0, ((1, 32),), jnp.float32),
        "currents_past": noise(keys[1], (LAGS, GROUPS, E, R), 1.0, 6.0, ((1, 32),)),
        "spectra_past": noise(keys[2], (LAGS, PARENTS, K, R), 1.5, 9.0, ((1, 32),)),
        "self_inverse": noise(keys[3], (GROUPS, E, E), (2 * E) ** -0.5, 0.25, ((0, 32),)),
        "near_blocks": noise(keys[4], (GROUPS, NEAR, LAGS, E, E), (2 * NEAR * LAGS * E) ** -0.5, 0.078125, ((0, 32),)),
        "neighbours": draw_neighbours(jax.random.fold_in(keys[13], 71), 0),
        "near_mask": set_ends((jax.random.randint(keys[6], (GROUPS, NEAR), 0, 4) < 3).astype(jnp.int32), jax.random.fold_in(keys[6], 1), 0, 1),
        "ray_out": noise(keys[7], (E, K), E ** -0.5, 0.375),
        "ray_in": noise(keys[8], (K, E), K ** -0.5, 0.1875),
        "child_shift": jnp.clip(jax.random.uniform(keys[9], (CH, K), jnp.float32, -1.0, 1.0), -1.0, 1.0),
        "far_sources": set_ends(jax.random.randint(keys[10], (PARENTS, F), 0, PARENTS), jax.random.fold_in(keys[10], 1), 0, PARENTS - 1).astype(jnp.int32),
        "far_delays": set_ends(jax.random.randint(keys[11], (PARENTS, F), 1, LAGS + 1), jax.random.fold_in(keys[11], 1), 1, LAGS).astype(jnp.int32),
        "translation": noise(keys[12], (PARENTS, F, K), (4 * F) ** -0.5, 0.75, ((2, 32),), jnp.float32),
    }


def near_field(near_blocks, neighbours, near_mask, history):
    def per_group(entries):
        group_blocks, neighbour_ids, live_slots = entries
        picked = jnp.stack([past[neighbour_ids] for past in history], axis=1)
        picked = picked.astype(jnp.float32) * live_slots.astype(jnp.float32)[:, None, None, None]
        return jnp.einsum('nlef,nlfr->er', group_blocks.astype(jnp.float32), picked)
    return lax.map(per_group, (near_blocks, neighbours, near_mask))


def translate(spectra_history, far_sources, far_delays, translation):
    stacked = jnp.stack(spectra_history)

    def per_parent(entries):
        weights, sources, delays = entries
        picked = stacked[delays - 1, sources].astype(jnp.float32)
        return jnp.sum(weights[:, :, None] * picked, axis=0).astype(jnp.bfloat16)
    return lax.map(per_parent, (translation, far_sources, far_delays))


def far_field(incoming, child_shift, ray_in):
    def per_parent(arriving):
        received = (child_shift[:, :, None] * arriving.astype(jnp.float32)).astype(jnp.bfloat16)
        return jnp.einsum('ke,ckr->cer', ray_in.astype(jnp.float32), received.astype(jnp.float32))
    fields = lax.map(per_parent, incoming)
    return fields.reshape(-1, fields.shape[2], fields.shape[3])


def outgoing(current, child_shift, ray_out):
    children = current.reshape(-1, child_shift.shape[0], current.shape[1], current.shape[2])

    def per_parent(members):
        spread = jnp.einsum('ek,cer->ckr', ray_out.astype(jnp.float32), members.astype(jnp.float32))
        return jnp.sum(child_shift[:, :, None] * spread, axis=0).astype(jnp.bfloat16)
    return lax.map(per_parent, children)


def solve(self_inverse, drive):
    def per_group(entries):
        inverse, column = entries
        return jnp.dot(inverse, column, preferred_element_type=jnp.float32).astype(jnp.bfloat16)
    return lax.map(per_group, (self_inverse, drive))


def reference(incident, currents_past, spectra_past, self_inverse, near_blocks, neighbours, near_mask, ray_out, ray_in, child_shift, far_sources, far_delays, translation):
    currents_history = [currents_past[lag_index] for lag_index in range(LAGS)]
    spectra_history = [spectra_past[lag_index] for lag_index in range(LAGS)]
    results = []
    for step_index in range(STEPS):
        near = near_field(near_blocks, neighbours, near_mask, currents_history)
        incoming = translate(spectra_history, far_sources, far_delays, translation)
        far = far_field(incoming, child_shift, ray_in)
        drive = (incident[step_index] - near - far).astype(jnp.bfloat16)
        current = solve(self_inverse, drive)
        results.append(current)
        if step_index + 1 < STEPS:
            spectra_history = [outgoing(current, child_shift, ray_out)] + spectra_history[:-1]
            currents_history = [current] + currents_history[:-1]
    return jnp.stack(results)
```

```python
import functools

import jax
import jax.numpy as jnp
from jax import lax
from jax.experimental import pallas as pl
from jax.experimental.pallas import tpu as pltpu
from jax.sharding import PartitionSpec as P

MESH = pl.DeviceIdType.MESH
TILE = 16
MIB = 1 << 20
AXES = ("grp", "dir")


def dot(a, b):
    return jnp.dot(a, b, preferred_element_type=jnp.float32)


def march(
    sizes,
    table,
    incident,
    currents_past,
    spectra_past,
    self_inverse,
    near_blocks,
    ray_out_t,
    ray_in_t,
    shift_rows,
    shift_columns,
    slots,
    factors,
    out,
    *scratch,
):
    steps, lags, devices, per_row, groups, near_slots, kept = sizes
    scratch = list(scratch)
    times = lags + steps - 1
    curs = [scratch.pop(0) for _ in range(times)]
    bands = [scratch.pop(0) for _ in range(times)]
    leaving = [scratch.pop(0) for _ in range(steps - 1)]
    turned = [scratch.pop(0) for _ in range(steps)]
    arrived = [scratch.pop(0) for _ in range(steps)]
    (last, inc, inverse, blocks, project, test, acc, part, weights) = scratch[:9]
    (load_sem, own_sem, cur_send, cur_recv, band_send, band_recv, inc_send, inc_recv, out_sem) = scratch[9:]
    padded = bands[0].shape[1]
    depth = padded // TILE
    parents = devices
    wide = parents * TILE
    chunk = 8
    me = lax.axis_index("grp") * per_row + lax.axis_index("dir")

    def place(device):
        return (device // per_row, device % per_row)

    loads = [
        pltpu.make_async_copy(near_blocks, blocks, load_sem.at[0]),
        pltpu.make_async_copy(incident, inc, load_sem.at[1]),
        pltpu.make_async_copy(self_inverse, inverse, load_sem.at[2]),
    ]
    for lag in range(lags):
        slot = lags - 1 - lag
        loads.append(
            pltpu.make_async_copy(
                currents_past.at[lag], curs[slot].at[pl.ds(groups, groups)], load_sem.at[3 + lag]
            )
        )
        loads.append(
            pltpu.make_async_copy(spectra_past.at[lag, me], bands[slot].at[me], own_sem.at[lag])
        )
    for load in loads[1:] + loads[:1]:
        load.start()

    barrier = pltpu.get_barrier_semaphore()

    def greet(offset, carry):
        device = lax.rem(me + offset, devices)
        pl.semaphore_signal(barrier, inc=1, device_id=place(device), device_id_type=MESH)
        return carry

    lax.fori_loop(1, devices, greet, 0)
    pl.semaphore_wait(barrier, devices - 1)

    def neighbour_copies(source, slot):
        def copy(side):
            device = me + (1 if side == 0 else -1)
            return pltpu.make_async_remote_copy(
                src_ref=source,
                dst_ref=curs[slot].at[pl.ds(0 if side == 0 else 2 * groups, groups)],
                send_sem=cur_send.at[slot, side],
                recv_sem=cur_recv.at[slot, side],
                device_id=place(device),
                device_id_type=MESH,
            )

        return copy

    def start_neighbours(source, slot):
        copy = neighbour_copies(source, slot)

        @pl.when(me < devices - 1)
        def _():
            copy(0).start()

        @pl.when(me > 0)
        def _():
            copy(1).start()

    def wait_neighbours(slot):
        own = curs[slot].at[pl.ds(groups, groups)]
        copy = neighbour_copies(own, slot)

        @pl.when(me > 0)
        def _():
            copy(0).wait_recv()

        @pl.when(me < devices - 1)
        def _():
            copy(1).wait_recv()

    def finish_neighbours(slot):
        own = curs[slot].at[pl.ds(groups, groups)]
        copy = neighbour_copies(own, slot)

        @pl.when(me < devices - 1)
        def _():
            copy(0).wait_send()

        @pl.when(me > 0)
        def _():
            copy(1).wait_send()

    def post(source, target, send, recv, device):
        pltpu.make_async_remote_copy(
            src_ref=source,
            dst_ref=target.at[me],
            send_sem=send,
            recv_sem=recv,
            device_id=place(device),
            device_id_type=MESH,
        ).start()

    def drain(buffer, sem):
        most = buffer.at[pl.ds(0, devices - 1)]
        pltpu.make_async_copy(most, most, sem).wait()

    for lag in reversed(range(lags)):
        slot = lags - 1 - lag

        def first(offset, carry, lag=lag, slot=slot):
            device = lax.rem(me + offset, devices)
            post(
                spectra_past.at[lag, device],
                bands[slot],
                band_send.at[slot],
                band_recv.at[slot],
                device,
            )
            return carry

        lax.fori_loop(1, devices, first, 0)
    for lag in reversed(range(lags)):
        start_neighbours(currents_past.at[lag], lags - 1 - lag)

    for cur in curs:
        cur[3 * groups] = jnp.zeros(cur.shape[1:], cur.dtype)

    def build(o):
        lane = lax.broadcasted_iota(jnp.int32, (slots.shape[1], lags * wide), 1)
        chosen = (lane // TILE == slots[o]).astype(jnp.float32).astype(jnp.bfloat16)
        full = dot(factors[o], chosen)
        row = lax.broadcasted_iota(jnp.int32, full.shape, 0) % TILE
        column = lax.broadcasted_iota(jnp.int32, full.shape, 1) % TILE
        return jnp.where(row == column, full, 0.0).astype(jnp.bfloat16)

    if kept:

        def build_one(o, carry):
            full = build(o)
            for tile in range(depth):
                for lag in range(lags):
                    weights[tile, lag, pl.ds(pl.multiple_of(o * TILE, TILE), TILE), :] = full[
                        tile * TILE : (tile + 1) * TILE, lag * wide : (lag + 1) * wide
                    ]
            return carry

        lax.fori_loop(0, parents, build_one, 0)

    children = shift_rows.shape[0]
    unknowns = ray_out_t.shape[1]

    def build_ray(band, carry):
        rows = pl.ds(pl.multiple_of(band * padded, TILE), padded)
        value = ray_out_t[rows, :].astype(jnp.float32)
        shifts = shift_columns[rows, :]
        for child in range(children):
            project[rows, child * unknowns : (child + 1) * unknowns] = (
                value * shifts[:, child : child + 1]
            ).astype(jnp.bfloat16)
        return carry

    lax.fori_loop(0, devices, build_ray, 0)

    def build_test(piece, carry):
        rows = pl.ds(pl.multiple_of(piece * 32, 32), 32)
        value = ray_in_t[rows, :].astype(jnp.float32)
        for child in range(children):
            test[child, rows, :] = (value * shift_rows[child : child + 1, :]).astype(jnp.bfloat16)
        return carry

    lax.fori_loop(0, unknowns // 32, build_test, 0)

    def near_part(slot, lag, step, opening):
        def one(g, carry):
            total = inc[step, g] if opening else acc[g]
            for n in range(near_slots):
                total = total - dot(blocks[g, n, lag], curs[slot][table[g, n]])
            acc[g] = total
            return carry

        lax.fori_loop(0, groups, one, 0)

    def band_rows(slot, tile):
        return bands[slot][:, tile * TILE : (tile + 1) * TILE, :].reshape(wide, bands[slot].shape[2])

    def translate(step, slots_used, lag, final):
        source = [band_rows(slots_used[lag], tile) for tile in range(depth)]

        def one(piece, carry):
            turn = lax.rem(me // chunk + piece, parents // chunk)
            first_o = turn * chunk
            rows = pl.ds(pl.multiple_of(first_o * TILE, TILE), chunk * TILE)
            if not kept:
                built = [build(first_o + o) for o in range(chunk)]
            for tile in range(depth):
                if kept:
                    weight = weights[tile, lag, rows, :]
                else:
                    weight = jnp.concatenate(
                        [
                            b[tile * TILE : (tile + 1) * TILE, lag * wide : (lag + 1) * wide]
                            for b in built
                        ],
                        axis=0,
                    )
                got = dot(weight, source[tile])
                if not final:
                    part[tile, rows, :] = got
                else:
                    got = (got + part[tile, rows, :]).astype(jnp.bfloat16)
                    turned[step][pl.ds(first_o, chunk), tile * TILE : (tile + 1) * TILE, :] = (
                        got.reshape(chunk, TILE, got.shape[1])
                    )
            if final:
                send_chunk(turned[step], arrived[step], inc_send.at[step], inc_recv.at[step], first_o)
            return carry

        lax.fori_loop(0, parents // chunk, one, 0)

    def send_chunk(source, target, send, recv, begin):
        def one(offset, carry):
            device = begin + lax.rem(me + offset, chunk)

            @pl.when(device != me)
            def _():
                post(source.at[device], target, send, recv, device)

            @pl.when(device == me)
            def _():
                target[me] = source[me]

            return carry

        lax.fori_loop(0, chunk, one, 0)

    def outgoing(step, slot):
        stacked = curs[slot][pl.ds(groups, groups)].reshape(children * unknowns, -1)

        def one(piece, carry):
            turn = lax.rem(me // chunk + piece, devices // chunk)
            begin = turn * chunk
            rows = pl.ds(pl.multiple_of(begin * padded, TILE), chunk * padded)
            got = dot(project[rows, :], stacked).astype(jnp.bfloat16)
            leaving[step][pl.ds(begin, chunk)] = got.reshape(chunk, padded, got.shape[1])
            send_chunk(leaving[step], bands[slot], band_send.at[slot], band_recv.at[slot], begin)
            return carry

        lax.fori_loop(0, devices // chunk, one, 0)

    for load in loads:
        load.wait()
    results = []
    for step in range(steps):
        newest = lags + step - 1
        oldest = newest - 1
        if step == 0:
            drain(bands[oldest], band_recv.at[oldest])
            wait_neighbours(oldest)
        near_part(oldest, 1, step, True)
        translate(step, [newest, oldest], 1, False)
        drain(bands[newest], band_recv.at[newest])
        translate(step, [newest, oldest], 0, True)
        wait_neighbours(newest)
        near_part(newest, 0, step, False)
        drain(arrived[step], inc_recv.at[step])
        slot = lags + step
        target, base = (curs[slot], groups) if step + 1 < steps else (last, 0)
        received = arrived[step][...].reshape(devices * padded, -1)

        def solve(g, carry, target=target, base=base, received=received):
            drive = (acc[g] - dot(test[g], received)).astype(jnp.bfloat16)
            target[base + g] = dot(inverse[g], drive).astype(jnp.bfloat16)
            return carry

        lax.fori_loop(0, groups, solve, 0)
        own = target.at[pl.ds(base, groups)]
        results.append(pltpu.make_async_copy(own, out.at[step], out_sem.at[step]))
        if step + 1 < steps:
            start_neighbours(own, slot)
            outgoing(step, slot)
        results[-1].start()
    for slot in range(times):
        drain(bands[slot], band_send.at[slot])
        finish_neighbours(slot)
        if slot == times - 1:
            pass
    for step in range(steps):
        drain(arrived[step], inc_send.at[step])
        results[step].wait()


def on_device(
    devices,
    per_row,
    incident,
    currents_past,
    spectra_past,
    self_inverse,
    near_blocks,
    neighbours,
    near_mask,
    ray_out,
    ray_in,
    child_shift,
    far_sources,
    far_delays,
    translation,
):
    steps, groups, unknowns, columns = incident.shape
    lags = currents_past.shape[0]
    near_slots = neighbours.shape[1]
    children, rays = child_shift.shape
    parents = far_sources.shape[0]
    band = rays // devices
    padded = -(-band // TILE) * TILE
    depth = padded // TILE
    wide = parents * TILE
    bf16 = jnp.bfloat16
    first_group = (lax.axis_index(AXES) - 1) * groups
    table = jnp.where(near_mask > 0, neighbours - first_group, 3 * groups)
    spread = ((0, 0), (0, padded - band), (0, 0))

    def by_band(rows):
        width = rows.shape[1]
        return jnp.pad(rows.reshape(devices, band, width), spread).reshape(devices * padded, width)

    ray_out_t = by_band(ray_out.T)
    ray_in_t = by_band(ray_in).T
    shift_columns = by_band(child_shift.T)
    shift_rows = shift_columns.T
    past = jnp.pad(
        spectra_past.reshape(lags, devices, band, columns),
        ((0, 0), (0, 0), (0, padded - band), (0, 0)),
    )
    slots = ((far_delays - 1) * parents + far_sources)[:, :, None]
    factors = jnp.pad(jnp.swapaxes(translation, 1, 2), spread).astype(bf16)
    kept = depth * lags * wide * wide * 2 <= 12 * MIB
    times = lags + steps - 1
    slabs = pltpu.VMEM((devices, padded, columns), bf16)
    scratch = (
        [pltpu.VMEM((3 * groups + 1, unknowns, columns), bf16)] * times
        + [slabs] * times
        + [slabs] * (steps - 1)
        + [slabs] * steps
        + [slabs] * steps
        + [
            pltpu.VMEM((groups, unknowns, columns), bf16),
            pltpu.VMEM(incident.shape, jnp.float32),
            pltpu.VMEM(self_inverse.shape, bf16),
            pltpu.VMEM(near_blocks.shape, bf16),
            pltpu.VMEM((devices * padded, children * unknowns), bf16),
            pltpu.VMEM((children, unknowns, devices * padded), bf16),
            pltpu.VMEM((groups, unknowns, columns), jnp.float32),
            pltpu.VMEM((depth, wide, columns), jnp.float32),
            pltpu.VMEM((depth, lags, wide, wide) if kept else (1, 1, TILE, 128), bf16),
            pltpu.SemaphoreType.DMA((3 + lags,)),
            pltpu.SemaphoreType.DMA((lags,)),
            pltpu.SemaphoreType.DMA((times, 2)),
            pltpu.SemaphoreType.DMA((times, 2)),
            pltpu.SemaphoreType.DMA((times,)),
            pltpu.SemaphoreType.DMA((times,)),
            pltpu.SemaphoreType.DMA((steps,)),
            pltpu.SemaphoreType.DMA((steps,)),
            pltpu.SemaphoreType.DMA((steps,)),
        ]
    )
    sizes = (steps, lags, devices, per_row, groups, near_slots, kept)
    far = pl.BlockSpec(memory_space=pl.ANY)
    near = pl.BlockSpec(memory_space=pltpu.VMEM)
    return pl.pallas_call(
        functools.partial(march, sizes),
        out_shape=jax.ShapeDtypeStruct(incident.shape, bf16),
        in_specs=[pl.BlockSpec(memory_space=pltpu.SMEM)] + [far] * 5 + [near] * 6,
        out_specs=far,
        scratch_shapes=scratch,
        compiler_params=pltpu.CompilerParams(
            collective_id=0, has_side_effects=True, vmem_limit_bytes=63 * MIB
        ),
    )(
        table,
        incident,
        currents_past,
        past,
        self_inverse,
        near_blocks,
        ray_out_t,
        ray_in_t,
        shift_rows,
        shift_columns,
        slots,
        factors,
    )


def solution(mesh):
    in_specs = (
        P(None, AXES, None, None),
        P(None, AXES, None, None),
        P(None, AXES, None, None),
        P(AXES, None, None),
        P(AXES, None, None, None, None),
        P(AXES, None),
        P(AXES, None),
        P(),
        P(),
        P(),
        P(),
        P(),
        P(None, None, AXES),
    )
    per_row = mesh.shape["dir"]
    devices = mesh.shape["grp"] * per_row
    return jax.shard_map(
        functools.partial(on_device, devices, per_row),
        mesh=mesh,
        in_specs=in_specs,
        out_specs=P(None, AXES, None, None),
        check_vma=False,
    )
```

```python
import functools

import jax
import jax.numpy as jnp
from jax import lax
from jax.experimental import pallas as pl
from jax.experimental.pallas import tpu as pltpu
from jax.sharding import PartitionSpec as P

MESH = pl.DeviceIdType.MESH
TILE = 16
MIB = 1 << 20
AXES = ("grp", "dir")


def dot(a, b):
    return jnp.dot(a, b, preferred_element_type=jnp.float32)


def march(
    sizes,
    table,
    incident,
    currents_past,
    spectra_past,
    self_inverse,
    near_blocks,
    ray_out_t,
    ray_in_t,
    shift_rows,
    shift_columns,
    slots,
    factors,
    out,
    *scratch,
):
    steps, lags, devices, per_row, groups, near_slots, kept = sizes
    scratch = list(scratch)
    times = lags + steps - 1
    curs = [scratch.pop(0) for _ in range(times)]
    bands = [scratch.pop(0) for _ in range(times)]
    leaving = [scratch.pop(0) for _ in range(steps - 1)]
    turned = [scratch.pop(0) for _ in range(steps)]
    arrived = [scratch.pop(0) for _ in range(steps)]
    (last, inc, inverse, blocks, project, test, acc, part, weights) = scratch[:9]
    (load_sem, own_sem, cur_send, cur_recv, band_send, band_recv, inc_send, inc_recv, out_sem) = scratch[9:]
    padded = bands[0].shape[1]
    depth = padded // TILE
    parents = devices
    wide = parents * TILE
    chunk = 16
    me = lax.axis_index("grp") * per_row + lax.axis_index("dir")

    def place(device):
        return (device // per_row, device % per_row)

    loads = [
        pltpu.make_async_copy(near_blocks, blocks, load_sem.at[0]),
        pltpu.make_async_copy(incident, inc, load_sem.at[1]),
        pltpu.make_async_copy(self_inverse, inverse, load_sem.at[2]),
    ]
    for lag in range(lags):
        slot = lags - 1 - lag
        loads.append(
            pltpu.make_async_copy(
                currents_past.at[lag], curs[slot].at[pl.ds(groups, groups)], load_sem.at[3 + lag]
            )
        )
        loads.append(
            pltpu.make_async_copy(spectra_past.at[lag, me], bands[slot].at[me], own_sem.at[lag])
        )
    for load in loads[1:] + loads[:1]:
        load.start()

    barrier = pltpu.get_barrier_semaphore()

    def greet(offset, carry):
        device = lax.rem(me + offset, devices)
        pl.semaphore_signal(barrier, inc=1, device_id=place(device), device_id_type=MESH)
        return carry

    lax.fori_loop(1, devices, greet, 0)
    pl.semaphore_wait(barrier, devices - 1)

    def neighbour_copies(source, slot):
        def copy(side):
            device = me + (1 if side == 0 else -1)
            return pltpu.make_async_remote_copy(
                src_ref=source,
                dst_ref=curs[slot].at[pl.ds(0 if side == 0 else 2 * groups, groups)],
                send_sem=cur_send.at[slot, side],
                recv_sem=cur_recv.at[slot, side],
                device_id=place(device),
                device_id_type=MESH,
            )

        return copy

    def start_neighbours(source, slot):
        copy = neighbour_copies(source, slot)

        @pl.when(me < devices - 1)
        def _():
            copy(0).start()

        @pl.when(me > 0)
        def _():
            copy(1).start()

    def wait_neighbours(slot):
        own = curs[slot].at[pl.ds(groups, groups)]
        copy = neighbour_copies(own, slot)

        @pl.when(me > 0)
        def _():
            copy(0).wait_recv()

        @pl.when(me < devices - 1)
        def _():
            copy(1).wait_recv()

    def finish_neighbours(slot):
        own = curs[slot].at[pl.ds(groups, groups)]
        copy = neighbour_copies(own, slot)

        @pl.when(me < devices - 1)
        def _():
            copy(0).wait_send()

        @pl.when(me > 0)
        def _():
            copy(1).wait_send()

    def post(source, target, send, recv, device):
        pltpu.make_async_remote_copy(
            src_ref=source,
            dst_ref=target.at[me],
            send_sem=send,
            recv_sem=recv,
            device_id=place(device),
            device_id_type=MESH,
        ).start()

    def drain(buffer, sem):
        most = buffer.at[pl.ds(0, devices - 1)]
        pltpu.make_async_copy(most, most, sem).wait()

    for lag in reversed(range(lags)):
        slot = lags - 1 - lag

        def first(offset, carry, lag=lag, slot=slot):
            device = lax.rem(me + offset, devices)
            post(
                spectra_past.at[lag, device],
                bands[slot],
                band_send.at[slot],
                band_recv.at[slot],
                device,
            )
            return carry

        lax.fori_loop(1, devices, first, 0)
    for lag in reversed(range(lags)):
        start_neighbours(currents_past.at[lag], lags - 1 - lag)

    for cur in curs:
        cur[3 * groups] = jnp.zeros(cur.shape[1:], cur.dtype)

    def build(o):
        lane = lax.broadcasted_iota(jnp.int32, (slots.shape[1], lags * wide), 1)
        chosen = (lane // TILE == slots[o]).astype(jnp.float32).astype(jnp.bfloat16)
        full = dot(factors[o], chosen)
        row = lax.broadcasted_iota(jnp.int32, full.shape, 0) % TILE
        column = lax.broadcasted_iota(jnp.int32, full.shape, 1) % TILE
        return jnp.where(row == column, full, 0.0).astype(jnp.bfloat16)

    if kept:

        def build_one(o, carry):
            full = build(o)
            for tile in range(depth):
                for lag in range(lags):
                    weights[tile, lag, pl.ds(pl.multiple_of(o * TILE, TILE), TILE), :] = full[
                        tile * TILE : (tile + 1) * TILE, lag * wide : (lag + 1) * wide
                    ]
            return carry

        lax.fori_loop(0, parents, build_one, 0)

    children = shift_rows.shape[0]
    unknowns = ray_out_t.shape[1]

    def build_ray(band, carry):
        rows = pl.ds(pl.multiple_of(band * padded, TILE), padded)
        value = ray_out_t[rows, :].astype(jnp.float32)
        shifts = shift_columns[rows, :]
        for child in range(children):
            project[rows, child * unknowns : (child + 1) * unknowns] = (
                value * shifts[:, child : child + 1]
            ).astype(jnp.bfloat16)
        return carry

    lax.fori_loop(0, devices, build_ray, 0)

    def build_test(piece, carry):
        rows = pl.ds(pl.multiple_of(piece * 32, 32), 32)
        value = ray_in_t[rows, :].astype(jnp.float32)
        for child in range(children):
            test[child, rows, :] = (value * shift_rows[child : child + 1, :]).astype(jnp.bfloat16)
        return carry

    lax.fori_loop(0, unknowns // 32, build_test, 0)

    def near_part(slot, lag, step, opening):
        def one(g, carry):
            total = inc[step, g] if opening else acc[g]
            for n in range(near_slots):
                total = total - dot(blocks[g, n, lag], curs[slot][table[g, n]])
            acc[g] = total
            return carry

        lax.fori_loop(0, groups, one, 0)

    def band_rows(slot, tile):
        return bands[slot][:, tile * TILE : (tile + 1) * TILE, :].reshape(wide, bands[slot].shape[2])

    def translate(step, slots_used, lag, final):
        source = [band_rows(slots_used[lag], tile) for tile in range(depth)]

        def one(piece, carry):
            turn = lax.rem(me // chunk + piece, parents // chunk)
            first_o = turn * chunk
            rows = pl.ds(pl.multiple_of(first_o * TILE, TILE), chunk * TILE)
            if not kept:
                built = [build(first_o + o) for o in range(chunk)]
            for tile in range(depth):
                if kept:
                    weight = weights[tile, lag, rows, :]
                else:
                    weight = jnp.concatenate(
                        [
                            b[tile * TILE : (tile + 1) * TILE, lag * wide : (lag + 1) * wide]
                            for b in built
                        ],
                        axis=0,
                    )
                got = dot(weight, source[tile])
                if not final:
                    part[tile, rows, :] = got
                else:
                    got = (got + part[tile, rows, :]).astype(jnp.bfloat16)
                    turned[step][pl.ds(first_o, chunk), tile * TILE : (tile + 1) * TILE, :] = (
                        got.reshape(chunk, TILE, got.shape[1])
                    )
            if final:
                send_chunk(turned[step], arrived[step], inc_send.at[step], inc_recv.at[step], first_o)
            return carry

        lax.fori_loop(0, parents // chunk, one, 0)

    def send_chunk(source, target, send, recv, begin):
        def one(offset, carry):
            device = begin + lax.rem(me + offset, chunk)

            @pl.when(device != me)
            def _():
                post(source.at[device], target, send, recv, device)

            @pl.when(device == me)
            def _():
                target[me] = source[me]

            return carry

        lax.fori_loop(0, chunk, one, 0)

    def outgoing(step, slot):
        stacked = curs[slot][pl.ds(groups, groups)].reshape(children * unknowns, -1)

        def one(piece, carry):
            turn = lax.rem(me // chunk + piece, devices // chunk)
            begin = turn * chunk
            rows = pl.ds(pl.multiple_of(begin * padded, TILE), chunk * padded)
            got = dot(project[rows, :], stacked).astype(jnp.bfloat16)
            leaving[step][pl.ds(begin, chunk)] = got.reshape(chunk, padded, got.shape[1])
            send_chunk(leaving[step], bands[slot], band_send.at[slot], band_recv.at[slot], begin)
            return carry

        lax.fori_loop(0, devices // chunk, one, 0)

    for load in loads:
        load.wait()
    results = []
    for step in range(steps):
        newest = lags + step - 1
        oldest = newest - 1
        if step == 0:
            drain(bands[oldest], band_recv.at[oldest])
            wait_neighbours(oldest)
        near_part(oldest, 1, step, True)
        translate(step, [newest, oldest], 1, False)
        drain(bands[newest], band_recv.at[newest])
        translate(step, [newest, oldest], 0, True)
        wait_neighbours(newest)
        near_part(newest, 0, step, False)
        drain(arrived[step], inc_recv.at[step])
        slot = lags + step
        target, base = (curs[slot], groups) if step + 1 < steps else (last, 0)
        received = arrived[step][...].reshape(devices * padded, -1)

        def solve(both, carry, target=target, base=base, received=received):
            tests = test[pl.ds(2 * both, 2)].reshape(2 * unknowns, received.shape[0])
            far = dot(tests, received)
            for half in range(2):
                g = 2 * both + half
                drive = acc[g] - far[half * unknowns : (half + 1) * unknowns]
                target[base + g] = dot(inverse[g], drive.astype(jnp.bfloat16)).astype(jnp.bfloat16)
            return carry

        lax.fori_loop(0, groups // 2, solve, 0)
        own = target.at[pl.ds(base, groups)]
        results.append(pltpu.make_async_copy(own, out.at[step], out_sem.at[step]))
        if step + 1 < steps:
            outgoing(step, slot)
            start_neighbours(own, slot)
        results[-1].start()
    for slot in range(times):
        drain(bands[slot], band_send.at[slot])
        finish_neighbours(slot)
    for step in range(steps):
        drain(arrived[step], inc_send.at[step])
        results[step].wait()


def on_device(
    devices,
    per_row,
    incident,
    currents_past,
    spectra_past,
    self_inverse,
    near_blocks,
    neighbours,
    near_mask,
    ray_out,
    ray_in,
    child_shift,
    far_sources,
    far_delays,
    translation,
):
    steps, groups, unknowns, columns = incident.shape
    lags = currents_past.shape[0]
    near_slots = neighbours.shape[1]
    children, rays = child_shift.shape
    parents = far_sources.shape[0]
    band = rays // devices
    padded = -(-band // TILE) * TILE
    depth = padded // TILE
    wide = parents * TILE
    bf16 = jnp.bfloat16
    first_group = (lax.axis_index(AXES) - 1) * groups
    table = jnp.where(near_mask > 0, neighbours - first_group, 3 * groups)
    spread = ((0, 0), (0, padded - band), (0, 0))

    def by_band(rows):
        width = rows.shape[1]
        return jnp.pad(rows.reshape(devices, band, width), spread).reshape(devices * padded, width)

    ray_out_t = by_band(ray_out.T)
    ray_in_t = by_band(ray_in).T
    shift_columns = by_band(child_shift.T)
    shift_rows = shift_columns.T
    past = jnp.pad(
        spectra_past.reshape(lags, devices, band, columns),
        ((0, 0), (0, 0), (0, padded - band), (0, 0)),
    )
    slots = ((far_delays - 1) * parents + far_sources)[:, :, None]
    factors = jnp.pad(jnp.swapaxes(translation, 1, 2), spread).astype(bf16)
    kept = depth * lags * wide * wide * 2 <= 12 * MIB
    times = lags + steps - 1
    slabs = pltpu.VMEM((devices, padded, columns), bf16)
    scratch = (
        [pltpu.VMEM((3 * groups + 1, unknowns, columns), bf16)] * times
        + [slabs] * times
        + [slabs] * (steps - 1)
        + [slabs] * steps
        + [slabs] * steps
        + [
            pltpu.VMEM((groups, unknowns, columns), bf16),
            pltpu.VMEM(incident.shape, jnp.float32),
            pltpu.VMEM(self_inverse.shape, bf16),
            pltpu.VMEM(near_blocks.shape, bf16),
            pltpu.VMEM((devices * padded, children * unknowns), bf16),
            pltpu.VMEM((children, unknowns, devices * padded), bf16),
            pltpu.VMEM((groups, unknowns, columns), jnp.float32),
            pltpu.VMEM((depth, wide, columns), jnp.float32),
            pltpu.VMEM((depth, lags, wide, wide) if kept else (1, 1, TILE, 128), bf16),
            pltpu.SemaphoreType.DMA((3 + lags,)),
            pltpu.SemaphoreType.DMA((lags,)),
            pltpu.SemaphoreType.DMA((times, 2)),
            pltpu.SemaphoreType.DMA((times, 2)),
            pltpu.SemaphoreType.DMA((times,)),
            pltpu.SemaphoreType.DMA((times,)),
            pltpu.SemaphoreType.DMA((steps,)),
            pltpu.SemaphoreType.DMA((steps,)),
            pltpu.SemaphoreType.DMA((steps,)),
        ]
    )
    sizes = (steps, lags, devices, per_row, groups, near_slots, kept)
    far = pl.BlockSpec(memory_space=pl.ANY)
    near = pl.BlockSpec(memory_space=pltpu.VMEM)
    return pl.pallas_call(
        functools.partial(march, sizes),
        out_shape=jax.ShapeDtypeStruct(incident.shape, bf16),
        in_specs=[pl.BlockSpec(memory_space=pltpu.SMEM)] + [far] * 5 + [near] * 6,
        out_specs=far,
        scratch_shapes=scratch,
        compiler_params=pltpu.CompilerParams(
            collective_id=0, has_side_effects=True, vmem_limit_bytes=63 * MIB
        ),
    )(
        table,
        incident,
        currents_past,
        past,
        self_inverse,
        near_blocks,
        ray_out_t,
        ray_in_t,
        shift_rows,
        shift_columns,
        slots,
        factors,
    )


def solution(mesh):
    in_specs = (
        P(None, AXES, None, None),
        P(None, AXES, None, None),
        P(None, AXES, None, None),
        P(AXES, None, None),
        P(AXES, None, None, None, None),
        P(AXES, None),
        P(AXES, None),
        P(),
        P(),
        P(),
        P(),
        P(),
        P(None, None, AXES),
    )
    per_row = mesh.shape["dir"]
    devices = mesh.shape["grp"] * per_row
    return jax.shard_map(
        functools.partial(on_device, devices, per_row),
        mesh=mesh,
        in_specs=in_specs,
        out_specs=P(None, AXES, None, None),
        check_vma=False,
    )
```

```python
import functools

import jax
import jax.numpy as jnp
from jax import lax
from jax.experimental import pallas as pl
from jax.experimental.pallas import tpu as pltpu
from jax.sharding import PartitionSpec as P

MESH = pl.DeviceIdType.MESH
TILE = 16
MIB = 1 << 20
AXES = ("grp", "dir")


def dot(a, b):
    return jnp.dot(a, b, preferred_element_type=jnp.float32)


def march(
    sizes,
    table,
    incident,
    currents_past,
    spectra_past,
    self_inverse,
    near_blocks,
    ray_out_t,
    ray_in_t,
    shift_rows,
    shift_columns,
    slots,
    factors,
    out,
    *scratch,
):
    steps, lags, devices, per_row, groups, near_slots, kept = sizes
    scratch = list(scratch)
    times = lags + steps - 1
    curs = [scratch.pop(0) for _ in range(times)]
    bands = [scratch.pop(0) for _ in range(times)]
    leaving = [scratch.pop(0) for _ in range(steps - 1)]
    turned = [scratch.pop(0) for _ in range(steps)]
    arrived = [scratch.pop(0) for _ in range(steps)]
    (last, inc, inverse, blocks, project, test, acc, part, weights) = scratch[:9]
    (load_sem, own_sem, cur_send, cur_recv, band_send, band_recv, inc_send, inc_recv, out_sem) = scratch[9:]
    padded = bands[0].shape[1]
    depth = padded // TILE
    parents = devices
    wide = parents * TILE
    chunk = 16
    me = lax.axis_index("grp") * per_row + lax.axis_index("dir")

    def place(device):
        return (device // per_row, device % per_row)

    loads = [
        pltpu.make_async_copy(near_blocks, blocks, load_sem.at[0]),
        pltpu.make_async_copy(incident, inc, load_sem.at[1]),
        pltpu.make_async_copy(self_inverse, inverse, load_sem.at[2]),
    ]
    for lag in range(lags):
        slot = lags - 1 - lag
        loads.append(
            pltpu.make_async_copy(
                currents_past.at[lag], curs[slot].at[pl.ds(groups, groups)], load_sem.at[3 + lag]
            )
        )
        loads.append(
            pltpu.make_async_copy(spectra_past.at[lag, me], bands[slot].at[me], own_sem.at[lag])
        )
    for load in loads[1:] + loads[:1]:
        load.start()

    barrier = pltpu.get_barrier_semaphore()

    def greet(offset, carry):
        device = lax.rem(me + offset, devices)
        pl.semaphore_signal(barrier, inc=1, device_id=place(device), device_id_type=MESH)
        return carry

    lax.fori_loop(1, devices, greet, 0)
    pl.semaphore_wait(barrier, devices - 1)

    def neighbour_copies(source, slot):
        def copy(side):
            device = me + (1 if side == 0 else -1)
            return pltpu.make_async_remote_copy(
                src_ref=source,
                dst_ref=curs[slot].at[pl.ds(0 if side == 0 else 2 * groups, groups)],
                send_sem=cur_send.at[slot, side],
                recv_sem=cur_recv.at[slot, side],
                device_id=place(device),
                device_id_type=MESH,
            )

        return copy

    def start_neighbours(source, slot):
        copy = neighbour_copies(source, slot)

        @pl.when(me < devices - 1)
        def _():
            copy(0).start()

        @pl.when(me > 0)
        def _():
            copy(1).start()

    def wait_neighbours(slot):
        own = curs[slot].at[pl.ds(groups, groups)]
        copy = neighbour_copies(own, slot)

        @pl.when(me > 0)
        def _():
            copy(0).wait_recv()

        @pl.when(me < devices - 1)
        def _():
            copy(1).wait_recv()

    def finish_neighbours(slot):
        own = curs[slot].at[pl.ds(groups, groups)]
        copy = neighbour_copies(own, slot)

        @pl.when(me < devices - 1)
        def _():
            copy(0).wait_send()

        @pl.when(me > 0)
        def _():
            copy(1).wait_send()

    def post(source, target, send, recv, device):
        pltpu.make_async_remote_copy(
            src_ref=source,
            dst_ref=target.at[me],
            send_sem=send,
            recv_sem=recv,
            device_id=place(device),
            device_id_type=MESH,
        ).start()

    def drain(buffer, sem):
        most = buffer.at[pl.ds(0, devices - 1)]
        pltpu.make_async_copy(most, most, sem).wait()

    for lag in reversed(range(lags)):
        slot = lags - 1 - lag

        def first(offset, carry, lag=lag, slot=slot):
            device = lax.rem(me + offset, devices)
            post(
                spectra_past.at[lag, device],
                bands[slot],
                band_send.at[slot],
                band_recv.at[slot],
                device,
            )
            return carry

        lax.fori_loop(1, devices, first, 0)
    for lag in reversed(range(lags)):
        start_neighbours(currents_past.at[lag], lags - 1 - lag)

    for cur in curs:
        cur[3 * groups] = jnp.zeros(cur.shape[1:], cur.dtype)

    def build(o):
        lane = lax.broadcasted_iota(jnp.int32, (slots.shape[1], lags * wide), 1)
        chosen = (lane // TILE == slots[o]).astype(jnp.float32).astype(jnp.bfloat16)
        full = dot(factors[o], chosen)
        row = lax.broadcasted_iota(jnp.int32, full.shape, 0) % TILE
        column = lax.broadcasted_iota(jnp.int32, full.shape, 1) % TILE
        return jnp.where(row == column, full, 0.0).astype(jnp.bfloat16)

    if kept:

        def build_one(o, carry):
            full = build(o)
            for tile in range(depth):
                for lag in range(lags):
                    weights[tile, lag, pl.ds(pl.multiple_of(o * TILE, TILE), TILE), :] = full[
                        tile * TILE : (tile + 1) * TILE, lag * wide : (lag + 1) * wide
                    ]
            return carry

        lax.fori_loop(0, parents, build_one, 0)

    children = shift_rows.shape[0]
    unknowns = ray_out_t.shape[1]

    def build_ray(band, carry):
        rows = pl.ds(pl.multiple_of(band * padded, TILE), padded)
        value = ray_out_t[rows, :].astype(jnp.float32)
        shifts = shift_columns[rows, :]
        for child in range(children):
            project[rows, child * unknowns : (child + 1) * unknowns] = (
                value * shifts[:, child : child + 1]
            ).astype(jnp.bfloat16)
        return carry

    lax.fori_loop(0, devices, build_ray, 0)

    def build_test(piece, carry):
        rows = pl.ds(pl.multiple_of(piece * 32, 32), 32)
        value = ray_in_t[rows, :].astype(jnp.float32)
        for child in range(children):
            test[child, rows, :] = (value * shift_rows[child : child + 1, :]).astype(jnp.bfloat16)
        return carry

    lax.fori_loop(0, unknowns // 32, build_test, 0)

    def near_part(slot, lag, step, opening):
        def one(g, carry):
            total = inc[step, g] if opening else acc[g]
            for n in range(near_slots):
                total = total - dot(blocks[g, n, lag], curs[slot][table[g, n]])
            acc[g] = total
            return carry

        lax.fori_loop(0, groups, one, 0)

    def band_rows(slot, tile):
        return bands[slot][:, tile * TILE : (tile + 1) * TILE, :].reshape(wide, bands[slot].shape[2])

    def translate(step, slots_used, lag, final):
        source = [band_rows(slots_used[lag], tile) for tile in range(depth)]

        def one(piece, carry):
            turn = lax.rem(me // chunk + piece, parents // chunk)
            first_o = turn * chunk
            rows = pl.ds(pl.multiple_of(first_o * TILE, TILE), chunk * TILE)
            if not kept:
                built = [build(first_o + o) for o in range(chunk)]
            for tile in range(depth):
                if kept:
                    weight = weights[tile, lag, rows, :]
                else:
                    weight = jnp.concatenate(
                        [
                            b[tile * TILE : (tile + 1) * TILE, lag * wide : (lag + 1) * wide]
                            for b in built
                        ],
                        axis=0,
                    )
                got = dot(weight, source[tile])
                if not final:
                    part[tile, rows, :] = got
                else:
                    got = (got + part[tile, rows, :]).astype(jnp.bfloat16)
                    turned[step][pl.ds(first_o, chunk), tile * TILE : (tile + 1) * TILE, :] = (
                        got.reshape(chunk, TILE, got.shape[1])
                    )
            if final:
                send_chunk(turned[step], arrived[step], inc_send.at[step], inc_recv.at[step], first_o)
            return carry

        lax.fori_loop(0, parents // chunk, one, 0)

    def send_chunk(source, target, send, recv, begin):
        def one(offset, carry):
            device = begin + lax.rem(me + offset, chunk)

            @pl.when(device != me)
            def _():
                post(source.at[device], target, send, recv, device)

            @pl.when(device == me)
            def _():
                target[me] = source[me]

            return carry

        lax.fori_loop(0, chunk, one, 0)

    def outgoing(step, slot):
        stacked = curs[slot][pl.ds(groups, groups)].reshape(children * unknowns, -1)

        def one(piece, carry):
            turn = lax.rem(me // chunk + piece, devices // chunk)
            begin = turn * chunk
            rows = pl.ds(pl.multiple_of(begin * padded, TILE), chunk * padded)
            got = dot(project[rows, :], stacked).astype(jnp.bfloat16)
            leaving[step][pl.ds(begin, chunk)] = got.reshape(chunk, padded, got.shape[1])
            send_chunk(leaving[step], bands[slot], band_send.at[slot], band_recv.at[slot], begin)
            return carry

        lax.fori_loop(0, devices // chunk, one, 0)

    for load in loads:
        load.wait()
    results = []
    for step in range(steps):
        newest = lags + step - 1
        oldest = newest - 1
        if step == 0:
            drain(bands[oldest], band_recv.at[oldest])
        else:
            near_part(oldest, 1, step, True)
        translate(step, [newest, oldest], 1, False)
        drain(bands[newest], band_recv.at[newest])
        translate(step, [newest, oldest], 0, True)
        if step == 0:
            wait_neighbours(oldest)
            near_part(oldest, 1, step, True)
        wait_neighbours(newest)
        near_part(newest, 0, step, False)
        drain(arrived[step], inc_recv.at[step])
        slot = lags + step
        target, base = (curs[slot], groups) if step + 1 < steps else (last, 0)
        received = arrived[step][...].reshape(devices * padded, -1)

        def solve(both, carry, target=target, base=base, received=received):
            tests = test[pl.ds(2 * both, 2)].reshape(2 * unknowns, received.shape[0])
            far = dot(tests, received)
            for half in range(2):
                g = 2 * both + half
                drive = acc[g] - far[half * unknowns : (half + 1) * unknowns]
                target[base + g] = dot(inverse[g], drive.astype(jnp.bfloat16)).astype(jnp.bfloat16)
            return carry

        lax.fori_loop(0, groups // 2, solve, 0)
        own = target.at[pl.ds(base, groups)]
        results.append(pltpu.make_async_copy(own, out.at[step], out_sem.at[step]))
        if step + 1 < steps:
            outgoing(step, slot)
            start_neighbours(own, slot)
        results[-1].start()
    for slot in range(times):
        drain(bands[slot], band_send.at[slot])
        finish_neighbours(slot)
    for step in range(steps):
        drain(arrived[step], inc_send.at[step])
        results[step].wait()


def on_device(
    devices,
    per_row,
    incident,
    currents_past,
    spectra_past,
    self_inverse,
    near_blocks,
    neighbours,
    near_mask,
    ray_out,
    ray_in,
    child_shift,
    far_sources,
    far_delays,
    translation,
):
    steps, groups, unknowns, columns = incident.shape
    lags = currents_past.shape[0]
    near_slots = neighbours.shape[1]
    children, rays = child_shift.shape
    parents = far_sources.shape[0]
    band = rays // devices
    padded = -(-band // TILE) * TILE
    depth = padded // TILE
    wide = parents * TILE
    bf16 = jnp.bfloat16
    first_group = (lax.axis_index(AXES) - 1) * groups
    table = jnp.where(near_mask > 0, neighbours - first_group, 3 * groups)
    spread = ((0, 0), (0, padded - band), (0, 0))

    def by_band(rows):
        width = rows.shape[1]
        return jnp.pad(rows.reshape(devices, band, width), spread).reshape(devices * padded, width)

    ray_out_t = by_band(ray_out.T)
    ray_in_t = by_band(ray_in).T
    shift_columns = by_band(child_shift.T)
    shift_rows = shift_columns.T
    past = jnp.pad(
        spectra_past.reshape(lags, devices, band, columns),
        ((0, 0), (0, 0), (0, padded - band), (0, 0)),
    )
    slots = ((far_delays - 1) * parents + far_sources)[:, :, None]
    factors = jnp.pad(jnp.swapaxes(translation, 1, 2), spread).astype(bf16)
    kept = depth * lags * wide * wide * 2 <= 12 * MIB
    times = lags + steps - 1
    slabs = pltpu.VMEM((devices, padded, columns), bf16)
    scratch = (
        [pltpu.VMEM((3 * groups + 1, unknowns, columns), bf16)] * times
        + [slabs] * times
        + [slabs] * (steps - 1)
        + [slabs] * steps
        + [slabs] * steps
        + [
            pltpu.VMEM((groups, unknowns, columns), bf16),
            pltpu.VMEM(incident.shape, jnp.float32),
            pltpu.VMEM(self_inverse.shape, bf16),
            pltpu.VMEM(near_blocks.shape, bf16),
            pltpu.VMEM((devices * padded, children * unknowns), bf16),
            pltpu.VMEM((children, unknowns, devices * padded), bf16),
            pltpu.VMEM((groups, unknowns, columns), jnp.float32),
            pltpu.VMEM((depth, wide, columns), jnp.float32),
            pltpu.VMEM((depth, lags, wide, wide) if kept else (1, 1, TILE, 128), bf16),
            pltpu.SemaphoreType.DMA((3 + lags,)),
            pltpu.SemaphoreType.DMA((lags,)),
            pltpu.SemaphoreType.DMA((times, 2)),
            pltpu.SemaphoreType.DMA((times, 2)),
            pltpu.SemaphoreType.DMA((times,)),
            pltpu.SemaphoreType.DMA((times,)),
            pltpu.SemaphoreType.DMA((steps,)),
            pltpu.SemaphoreType.DMA((steps,)),
            pltpu.SemaphoreType.DMA((steps,)),
        ]
    )
    sizes = (steps, lags, devices, per_row, groups, near_slots, kept)
    far = pl.BlockSpec(memory_space=pl.ANY)
    near = pl.BlockSpec(memory_space=pltpu.VMEM)
    return pl.pallas_call(
        functools.partial(march, sizes),
        out_shape=jax.ShapeDtypeStruct(incident.shape, bf16),
        in_specs=[pl.BlockSpec(memory_space=pltpu.SMEM)] + [far] * 5 + [near] * 6,
        out_specs=far,
        scratch_shapes=scratch,
        compiler_params=pltpu.CompilerParams(
            collective_id=0, has_side_effects=True, vmem_limit_bytes=63 * MIB
        ),
    )(
        table,
        incident,
        currents_past,
        past,
        self_inverse,
        near_blocks,
        ray_out_t,
        ray_in_t,
        shift_rows,
        shift_columns,
        slots,
        factors,
    )


def solution(mesh):
    in_specs = (
        P(None, AXES, None, None),
        P(None, AXES, None, None),
        P(None, AXES, None, None),
        P(AXES, None, None),
        P(AXES, None, None, None, None),
        P(AXES, None),
        P(AXES, None),
        P(),
        P(),
        P(),
        P(),
        P(),
        P(None, None, AXES),
    )
    per_row = mesh.shape["dir"]
    devices = mesh.shape["grp"] * per_row
    return jax.shard_map(
        functools.partial(on_device, devices, per_row),
        mesh=mesh,
        in_specs=in_specs,
        out_specs=P(None, AXES, None, None),
        check_vma=False,
    )
```
